128 devices in a mesh: off: 4 (over y), tm: 32 (over x, z, core).
Axes of the slice: x: 4, y: 4, z: 4, core: 2. Of those that a mesh axis runs over, the one named last changes fastest.
Arguments:
- data: bfloat16 [524288, 1024], P('tm', 'off'), may hold values from -6 to 6
- leaf_basis: bfloat16 [4096, 64, 128], P('tm'), may hold values from -0.5 to 0.5
- level_weights: bfloat16 [12, 4096, 64, 128], P(None, 'tm'), may hold values from -0.5 to 0.5
- slowness_table: bfloat16 [1024, 1024], replicated, may hold values from -0.1875 to 0.1875
- model_basis: bfloat16 [4096, 64, 128], P('tm'), may hold values from -0.75 to 0.75
Outputs:
- model: bfloat16 [524288, 1024], P('tm', 'off')
The draws below stay inside these ranges and needn't reach their ends.
All inputs are finite; a program needn't handle non-finite values.
Results may differ from the reference program's by a relative error of at most 0.03.
Values may be sent and summed in bfloat16 or wider, within the bound.
A program may use at most 192 MiB of HBM per device.

```python
import jax
import jax.numpy as jnp

R2 = 64
TB = 128
NO = 1024
NP = 1024
LEVELS = 12
NB = 4096
NT = 524288


def block_levels(own_key, extent, shards, least, largest):
    def one(axis_at, parts):
        draws = jax.random.uniform(jax.random.fold_in(jax.random.fold_in(own_key, 6), axis_at), (parts,), jnp.float32, least / len(shards), largest / len(shards))
        return jnp.repeat(jnp.exp(draws), extent[axis_at] // parts).reshape((-1,) + (1,) * (len(extent) - axis_at - 1))

    level = one(*shards[0])
    for cut in shards[1:]:
        level = level * one(*cut)
    return level


def centred(rng, shape, spread, limit, pieces=(), dtype=jnp.bfloat16):
    values = jax.random.normal(rng, shape, jnp.float32) * spread
    if len(pieces) > 0:
        values = block_levels(rng, shape, pieces, -0.22, 0.18) * values
    return jnp.clip(values, min=-limit, max=limit).astype(dtype)


def setup_inputs(seed: int = 0) -> dict:
    seeds = jax.random.split(jax.random.key(seed), 6)
    data = centred(seeds[0], (NT, NO), 1.0, 6.0, ((0, 32), (1, 4)))
    leaf_basis = centred(seeds[1], (NB, R2, TB), TB ** -0.5, 0.5, ((0, 32),))
    level_weights = centred(seeds[2], (LEVELS, NB, R2, 2 * R2), (2 * R2) ** -0.5, 0.5, ((1, 32),))
    slowness_table = centred(seeds[3], (NO, NP), NO ** -0.5, 0.1875)
    model_basis = centred(seeds[4], (NB, R2, TB), R2 ** -0.5, 0.75, ((0, 32),))
    return {"data": data, "leaf_basis": leaf_basis, "level_weights": level_weights, "slowness_table": slowness_table, "model_basis": model_basis}


def apply_level(coeffs, level_w, spacing):
    count, rank, cols = coeffs.shape
    grouped = coeffs.reshape(count // (2 * spacing), 2, spacing, rank, cols)
    partner = grouped[:, ::-1].reshape(coeffs.shape)
    stacked = jnp.concatenate([coeffs, partner], axis=1)
    mixed = jnp.einsum('bkr,brn->bkn', level_w.astype(jnp.float32), stacked.astype(jnp.float32))
    return mixed.astype(jnp.bfloat16)


def reference(data, leaf_basis, level_weights, slowness_table, model_basis):
    blocks = data.reshape(NB, TB, NO)
    coeffs = jnp.einsum('brt,btn->brn', leaf_basis.astype(jnp.float32), blocks.astype(jnp.float32)).astype(jnp.bfloat16)
    for level in range(LEVELS):
        coeffs = apply_level(coeffs, level_weights[level], 2 ** level)
    slow = jnp.einsum('brn,np->pbr', coeffs.astype(jnp.float32), slowness_table.astype(jnp.float32)).astype(jnp.bfloat16)
    model = jnp.einsum('brt,pbr->btp', model_basis.astype(jnp.float32), slow.astype(jnp.float32))
    return model.reshape(NT, NP).astype(jnp.bfloat16)
```

```python
import functools

import jax
import jax.numpy as jnp
from jax import lax
from jax.experimental import pallas as pl
from jax.experimental.pallas import tpu as pltpu
from jax.sharding import PartitionSpec as P

MESH = pl.DeviceIdType.MESH
F32, BF16 = jnp.float32, jnp.bfloat16
CHUNKS = 8
RING = 4
GROUPS = RING * RING
R2, TB, COLS = 64, 128, 256


def place():
    y, tm = lax.axis_index("off"), lax.axis_index("tm")
    return y, tm // 8, (tm // 2) % 4, tm % 2


def device(y, x, z, core):
    return (y, x * 8 + z * 2 + core)


def dot(a, b):
    return jnp.dot(a, b, preferred_element_type=F32)


def pair_weight(own, partner):
    swapped = jnp.concatenate([partner[:, R2:], partner[:, :R2]], axis=1)
    return jnp.concatenate([own, swapped], axis=0)


def mix(weight, low, high):
    out = dot(weight, jnp.concatenate([low, high], axis=0)).astype(BF16)
    return out[:R2], out[R2:]


def signal_all(y, x, z, core):
    barrier = pltpu.get_barrier_semaphore()

    def tell(*there):
        pl.semaphore_signal(barrier, inc=1, device_id=device(*there), device_id_type=MESH)

    tell(y, x, z, 1 - core)
    for d in range(1, GROUPS):
        tell((y + d // RING) % RING, x, (z + d % RING) % RING, core)
    for d in range(1, RING):
        tell(y, (x + d) % RING, z, core)
    for dy in range(RING):
        for d in range(RING):
            source_z = (z + d) % RING
            if dy == 0 and d == 0:
                continue
            pl.when(x != z)(functools.partial(tell, (y + dy) % RING, z, source_z, core))
        for d in range(1, RING):
            there = (x + d) % RING
            new = (x != z) & (there != z)
            if dy > 0:
                new = new | (x == z)
            pl.when(new)(functools.partial(tell, (y + dy) % RING, there, x, core))
    pl.semaphore_wait(barrier, jnp.where(x == z, 28, 42))


def main_kernel(
    data, leaf, weights, table, out,
    data_v, leaf_v, w_v, table_v, c_v, sib_v, e_v, z_v, x_v, s_v, wz_v, wx_v,
    data_sem, leaf_sem, w_sem, table_sem, wz_send, wz_recv, wx_send, wx_recv,
    core_send, core_recv, z_send, z_recv, x_send, x_recv, back_send, back_recv,
):
    y, x, z, core = place()
    per = GROUPS // CHUNKS

    def load_data(p):
        return pltpu.make_async_copy(data.at[pl.ds(p * per, per)], data_v.at[pl.ds(p * per, per)], data_sem.at[p])

    def load_leaf(p):
        return pltpu.make_async_copy(leaf.at[pl.ds(p * per, per)], leaf_v.at[pl.ds(p * per, per)], leaf_sem.at[p])

    def load_w(level):
        return pltpu.make_async_copy(weights.at[level], w_v.at[level], w_sem.at[level])

    load_table = pltpu.make_async_copy(table, table_v, table_sem)
    for p in range(CHUNKS):
        load_leaf(p).start()
        load_data(p).start()
    for level in range(8):
        load_w(level).start()
    load_table.start()

    signal_all(y, x, z, core)

    def remote(src, dst, send, recv, there):
        return pltpu.make_async_remote_copy(
            src_ref=src, dst_ref=dst, send_sem=send, recv_sem=recv, device_id=device(*there), device_id_type=MESH
        )

    for d in range(1, RING):
        to = (z + d) % RING
        remote(weights.at[pl.ds(8, 2), RING * y + to], wz_v.at[z], wz_send, wz_recv, (y, x, to, core)).start()
    pltpu.make_async_copy(weights.at[pl.ds(8, 2), RING * y + z], wz_v.at[z], wz_recv).start()
    for d in range(RING):
        to = (z + d) % RING
        src = weights.at[pl.ds(10, 2), RING * y + to]

        def send_wx(src=src, to=to):
            remote(src, wx_v.at[x], wx_send, wx_recv, (y, z, to, core)).start()

        if d == 0:
            pl.when(x != z)(send_wx)

            @pl.when(x == z)
            def _():
                pltpu.make_async_copy(src, wx_v.at[x], wx_recv).start()
        else:
            send_wx()

    def leaf_part(p, carry):
        load_leaf(p).wait()
        load_data(p).wait()

        def some(j, carry):
            for u in range(4):
                n = j * 4 + u
                a, k = p * per + n // CHUNKS, n % CHUNKS
                c_v[a, k] = dot(leaf_v[a, k], data_v[a, k]).astype(BF16)
            return carry

        return lax.fori_loop(0, per * CHUNKS // 4, some, carry)

    lax.fori_loop(0, CHUNKS, leaf_part, 0)

    def mix_blocks(level, low, high):
        weight = pair_weight(w_v[(level, *low)], w_v[(level, *high)])
        c_v[low], c_v[high] = mix(weight, c_v[low], c_v[high])

    for level in range(6):
        load_w(level).wait()
        spacing = 2**level

        def some(j, carry, level=level, spacing=spacing):
            for u in range(4):
                n = j * 4 + u
                low = (n // spacing) * (2 * spacing) + n % spacing
                high = low + spacing
                mix_blocks(level, (low // CHUNKS, low % CHUNKS), (high // CHUNKS, high % CHUNKS))
            return carry

        lax.fori_loop(0, 16, some, 0)
    load_w(6).wait()
    load_w(7).wait()

    def send_core(k):
        return remote(c_v.at[:, k], sib_v.at[:, k], core_send.at[k], core_recv.at[k], (y, x, z, 1 - core))

    def level_6(k):
        def some(j, carry):
            for u in range(4):
                a = j * 4 + u
                mix_blocks(6, (a, k), (a + GROUPS // 2, k))
            return carry

        lax.fori_loop(0, GROUPS // 8, some, 0)
        send_core(k).start()

    def level_7(k):
        send_core(k).wait_recv()

        def some(j, carry):
            for u in range(4):
                a = j * 4 + u
                stacked = jnp.concatenate([c_v[a, k], sib_v[a, k]], axis=0)
                e_v[a, k] = dot(w_v[7, a, k], stacked).astype(BF16)
            return carry

        lax.fori_loop(0, GROUPS // 4, some, 0)
        for d in (5, 7, 13, 15, 1, 3, 4, 12, 6, 9, 11, 14, 2, 8, 10):
            ty, tz = (y + d // RING) % RING, (z + d % RING) % RING
            remote(e_v.at[RING * ty + tz, k], z_v.at[k, y, z], z_send.at[k], z_recv.at[k], (ty, x, tz, core)).start()
        pltpu.make_async_copy(e_v.at[RING * y + z, k], z_v.at[k, y, z], z_recv.at[k]).start()

    def two_levels(k, w, get, put):
        first = [pair_weight(w[b, 0, k], w[b + 1, 0, k]) for b in (0, 2)]
        second = [pair_weight(w[b, 1, k], w[b + 2, 1, k]) for b in (0, 1)]
        for q in range(RING):
            b0, b1 = mix(first[0], get(0, q), get(1, q))
            b2, b3 = mix(first[1], get(2, q), get(3, q))
            b0, b2 = mix(second[0], b0, b2)
            b1, b3 = mix(second[1], b1, b3)
            for b, value in enumerate((b0, b1, b2, b3)):
                put(b, q, value)

    def levels_z(k):
        pltpu.make_async_copy(z_v.at[k], z_v.at[k], z_recv.at[k]).wait()

        def put(b, q, value):
            z_v[k, q, b] = value

        two_levels(k, wz_v, lambda b, q: z_v[k, q, b], put)
        for d in (1, 3, 2):
            to = (x + d) % RING
            remote(z_v.at[k, :, to], x_v.at[k, x], x_send.at[k], x_recv.at[k], (y, to, z, core)).start()
        pltpu.make_async_copy(z_v.at[k, :, x], x_v.at[k, x], x_recv.at[k]).start()

    def levels_x(k):
        pltpu.make_async_copy(x_v.at[k], x_v.at[k], x_recv.at[k]).wait()

        def put(b, q, value):
            x_v[k, b, q] = value

        two_levels(k, wx_v, lambda b, q: x_v[k, b, q], put)
        for part in range(RING):
            total = jnp.zeros((RING * R2, COLS), F32)
            for q in range(RING):
                rows = x_v[k, :, q].reshape(RING * R2, COLS)
                total += dot(rows, table_v[pl.ds(q * COLS, COLS), pl.ds(part * COLS, COLS)])
            s_v[k, :, part] = total.astype(BF16).reshape(RING, R2, COLS)
        mine = RING * y + z
        for d in (5, 7, 13, 15, 1, 3, 4, 12, 6, 9, 11, 14, 2, 8, 10, 0):
            ty, tx = (y + d // RING) % RING, (x + d % RING) % RING

            def send_back(ty=ty, tx=tx):
                remote(s_v.at[k, tx, ty], out.at[mine, k], back_send.at[k], back_recv.at[k], (ty, tx, x, core)).start()

            if d == 0:
                pl.when(x != z)(send_back)

                @pl.when(x == z)
                def _():
                    pltpu.make_async_copy(s_v.at[k, x, y], out.at[mine, k], back_recv.at[k]).start()
            else:
                send_back()

    def step(t, carry):
        pl.when(t < CHUNKS)(lambda: level_6(t))
        pl.when((t >= 1) & (t < CHUNKS + 1))(lambda: level_7(t - 1))

        @pl.when(t == 2)
        def _():
            pltpu.make_async_copy(wz_v, wz_v, wz_recv).wait()

        pl.when((t >= 2) & (t < CHUNKS + 2))(lambda: levels_z(t - 2))

        @pl.when(t == 3)
        def _():
            pltpu.make_async_copy(wx_v, wx_v, wx_recv).wait()
            load_table.wait()

        pl.when(t >= 3)(lambda: levels_x(t - 3))
        return carry

    lax.fori_loop(0, CHUNKS + 3, step, 0)

    def finish(k, carry):
        send_core(k).wait_send()
        pltpu.make_async_copy(e_v.at[pl.ds(0, 15), k], e_v.at[pl.ds(0, 15), k], z_send.at[k]).wait()
        pltpu.make_async_copy(x_v.at[k, pl.ds(0, 3)], x_v.at[k, pl.ds(0, 3)], x_send.at[k]).wait()

        @pl.when(x != z)
        def _():
            pltpu.make_async_copy(s_v.at[k], s_v.at[k], back_send.at[k]).wait()

        @pl.when(x == z)
        def _():
            pltpu.make_async_copy(e_v.at[pl.ds(0, 15), k], e_v.at[pl.ds(0, 15), k], back_send.at[k]).wait()

        pltpu.make_async_copy(out.at[:, k], out.at[:, k], back_recv.at[k]).wait()
        return carry

    lax.fori_loop(0, CHUNKS, finish, 0)
    pltpu.make_async_copy(wz_v.at[pl.ds(0, 3)], wz_v.at[pl.ds(0, 3)], wz_send).wait()

    @pl.when(x != z)
    def _():
        pltpu.make_async_copy(wx_v, wx_v, wx_send).wait()

    @pl.when(x == z)
    def _():
        pltpu.make_async_copy(wx_v.at[pl.ds(0, 3)], wx_v.at[pl.ds(0, 3)], wx_send).wait()


def model_kernel(basis, slow, out):
    def some(j, carry):
        for u in range(4):
            n = j * 4 + u
            rows = lax.dot_general(basis[n], slow[n], (((0,), (0,)), ((), ())), preferred_element_type=F32)
            out[n] = rows.astype(BF16)
        return carry

    lax.fori_loop(0, basis.shape[0] // 4, some, 0)


def local(data, leaf_basis, level_weights, slowness_table, model_basis):
    any_space = pl.BlockSpec(memory_space=pl.ANY)
    levels = level_weights.shape[0]
    dma, vmem = pltpu.SemaphoreType.DMA, pltpu.VMEM
    slow = pl.pallas_call(
        main_kernel,
        out_shape=jax.ShapeDtypeStruct((GROUPS, CHUNKS, R2, COLS), BF16),
        in_specs=[any_space] * 4,
        out_specs=any_space,
        scratch_shapes=[
            vmem((GROUPS, CHUNKS, TB, COLS), BF16),
            vmem((GROUPS, CHUNKS, R2, TB), BF16),
            vmem((8, GROUPS, CHUNKS, R2, TB), BF16),
            vmem(slowness_table.shape, BF16),
            vmem((GROUPS, CHUNKS, R2, COLS), BF16),
            vmem((GROUPS, CHUNKS, R2, COLS), BF16),
            vmem((GROUPS, CHUNKS, R2, COLS), BF16),
            vmem((CHUNKS, RING, RING, R2, COLS), BF16),
            vmem((CHUNKS, RING, RING, R2, COLS), BF16),
            vmem((CHUNKS, RING, RING, R2, COLS), BF16),
            vmem((RING, 2, CHUNKS, R2, TB), BF16),
            vmem((RING, 2, CHUNKS, R2, TB), BF16),
            dma((CHUNKS,)), dma((CHUNKS,)), dma((8,)), dma,
            dma, dma, dma, dma,
            dma((CHUNKS,)), dma((CHUNKS,)), dma((CHUNKS,)), dma((CHUNKS,)),
            dma((CHUNKS,)), dma((CHUNKS,)), dma((CHUNKS,)), dma((CHUNKS,)),
        ],
        compiler_params=pltpu.CompilerParams(collective_id=0, has_side_effects=True, vmem_limit_bytes=58 << 20),
    )(
        data.reshape(GROUPS, CHUNKS, TB, COLS),
        leaf_basis.reshape(GROUPS, CHUNKS, R2, TB),
        level_weights.reshape(levels, GROUPS, CHUNKS, R2, TB),
        slowness_table,
    )
    blocks = GROUPS * CHUNKS
    step = 16
    model = pl.pallas_call(
        model_kernel,
        grid=(blocks // step,),
        out_shape=jax.ShapeDtypeStruct((blocks, TB, COLS), BF16),
        in_specs=[
            pl.BlockSpec((step, R2, TB), lambda n: (n, 0, 0)),
            pl.BlockSpec((step, R2, COLS), lambda n: (n, 0, 0)),
        ],
        out_specs=pl.BlockSpec((step, TB, COLS), lambda n: (n, 0, 0)),
        compiler_params=pltpu.CompilerParams(vmem_limit_bytes=24 << 20),
    )(model_basis, slow.reshape(blocks, R2, COLS))
    return model.reshape(blocks * TB, COLS)


def solution(mesh):
    placed = (
        P("tm", "off"),
        P("tm", None, None),
        P(None, "tm", None, None),
        P(),
        P("tm", None, None),
    )
    return jax.shard_map(local, mesh=mesh, in_specs=placed, out_specs=P("tm", "off"), check_vma=False)
```

```python
import functools

import jax
import jax.numpy as jnp
from jax import lax
from jax.experimental import pallas as pl
from jax.experimental.pallas import tpu as pltpu
from jax.sharding import PartitionSpec as P

MESH = pl.DeviceIdType.MESH
F32, BF16 = jnp.float32, jnp.bfloat16
CHUNKS = 8
RING = 4
GROUPS = RING * RING
BATCH = 8
R2, TB, COLS = 64, 128, 256


def place():
    y, tm = lax.axis_index("off"), lax.axis_index("tm")
    return y, tm // 8, (tm // 2) % 4, tm % 2


def device(y, x, z, core):
    return (y, x * 8 + z * 2 + core)


def dot(a, b):
    return jnp.dot(a, b, preferred_element_type=F32)


def pair_weight(own, partner):
    swapped = jnp.concatenate([partner[:, R2:], partner[:, :R2]], axis=1)
    return jnp.concatenate([own, swapped], axis=0)


def mix(weight, low, high):
    out = dot(weight, jnp.concatenate([low, high], axis=0)).astype(BF16)
    return out[:R2], out[R2:]


def signal_all(y, x, z, core):
    barrier = pltpu.get_barrier_semaphore()

    def tell(*there):
        pl.semaphore_signal(barrier, inc=1, device_id=device(*there), device_id_type=MESH)

    tell(y, x, z, 1 - core)
    for d in range(1, GROUPS):
        tell((y + d // RING) % RING, x, (z + d % RING) % RING, core)
    for d in range(1, RING):
        tell(y, (x + d) % RING, z, core)
    for dy in range(RING):
        for d in range(RING):
            source_z = (z + d) % RING
            if dy == 0 and d == 0:
                continue
            pl.when(x != z)(functools.partial(tell, (y + dy) % RING, z, source_z, core))
        for d in range(1, RING):
            there = (x + d) % RING
            new = (x != z) & (there != z)
            if dy > 0:
                new = new | (x == z)
            pl.when(new)(functools.partial(tell, (y + dy) % RING, there, x, core))
    pl.semaphore_wait(barrier, jnp.where(x == z, 28, 42))


def main_kernel(
    data, leaf, weights, table, out,
    data_v, leaf_v, w_v, table_v, c_v, sib_v, e_v, z_v, x_v, s_v, wy_v, wz_v, wx_v,
    data_sem, leaf_sem, w_sem, table_sem, wy_send, wy_recv, wz_send, wz_recv, wx_send, wx_recv,
    core_send, core_recv, z_send, z_recv, x_send, x_recv, back_send, back_recv,
):
    y, x, z, core = place()
    per = GROUPS // CHUNKS

    def load_data(p):
        return pltpu.make_async_copy(data.at[pl.ds(p * per, per)], data_v.at[pl.ds(p * per, per)], data_sem.at[p])

    def load_leaf(p):
        return pltpu.make_async_copy(leaf.at[pl.ds(p * per, per)], leaf_v.at[pl.ds(p * per, per)], leaf_sem.at[p])

    def load_w(level):
        return pltpu.make_async_copy(weights.at[level], w_v.at[level], w_sem.at[level])

    load_table = pltpu.make_async_copy(table, table_v, table_sem)
    for p in range(CHUNKS):
        load_leaf(p).start()
        load_data(p).start()
    for level in range(8):
        load_w(level).start()
    load_table.start()

    signal_all(y, x, z, core)

    def remote(src, dst, send, recv, there):
        return pltpu.make_async_remote_copy(
            src_ref=src, dst_ref=dst, send_sem=send, recv_sem=recv, device_id=device(*there), device_id_type=MESH
        )

    for first, dst, send, recv in ((10, wy_v, wy_send, wy_recv), (8, wz_v, wz_send, wz_recv)):
        for d in (1, 3, 2):
            to = (z + d) % RING
            remote(weights.at[pl.ds(first, 2), RING * y + to], dst.at[z], send, recv, (y, x, to, core)).start()
        pltpu.make_async_copy(weights.at[pl.ds(first, 2), RING * y + z], dst.at[z], recv).start()

    def forward_weights():
        pltpu.make_async_copy(wy_v, wy_v, wy_recv).wait()
        for d in (1, 3, 2):
            to = (x + d) % RING
            remote(wy_v.at[to], wx_v.at[x], wx_send, wx_recv, (y, to, z, core)).start()
        pltpu.make_async_copy(wy_v.at[x], wx_v.at[x], wx_recv).start()

    def leaf_part(p, carry):
        load_leaf(p).wait()
        load_data(p).wait()

        def some(j, carry):
            a = p * per + j
            parts = [dot(leaf_v[a, k], data_v[a, k]).astype(BF16) for k in range(CHUNKS)]
            for k in range(CHUNKS):
                c_v[a, k] = parts[k]
            return carry

        return lax.fori_loop(0, per, some, carry)

    lax.fori_loop(0, CHUNKS, leaf_part, 0)

    def mix_blocks(level, pairs):
        mixed = [
            mix(pair_weight(w_v[(level, *low)], w_v[(level, *high)]), c_v[low], c_v[high]) for low, high in pairs
        ]
        for (low, high), (first, second) in zip(pairs, mixed):
            c_v[low], c_v[high] = first, second

    for level in range(6):
        load_w(level).wait()
        spacing = 2**level

        def some(j, carry, level=level, spacing=spacing):
            pairs = []
            for u in range(BATCH):
                n = j * BATCH + u
                low = (n // spacing) * (2 * spacing) + n % spacing
                high = low + spacing
                pairs.append(((low // CHUNKS, low % CHUNKS), (high // CHUNKS, high % CHUNKS)))
            mix_blocks(level, pairs)
            return carry

        lax.fori_loop(0, GROUPS * CHUNKS // 2 // BATCH, some, 0)
    load_w(6).wait()
    load_w(7).wait()
    forward_weights()

    def send_core(k):
        return remote(c_v.at[:, k], sib_v.at[:, k], core_send.at[k], core_recv.at[k], (y, x, z, 1 - core))

    def level_6(k):
        mix_blocks(6, [((a, k), (a + GROUPS // 2, k)) for a in range(GROUPS // 2)])
        send_core(k).start()

    def level_7(k):
        send_core(k).wait_recv()

        mixed = [
            dot(w_v[7, a, k], jnp.concatenate([c_v[a, k], sib_v[a, k]], axis=0)).astype(BF16) for a in range(GROUPS)
        ]
        for a in range(GROUPS):
            e_v[a, k] = mixed[a]
        for d in (5, 7, 13, 15, 1, 3, 4, 12, 6, 9, 11, 14, 2, 8, 10):
            ty, tz = (y + d // RING) % RING, (z + d % RING) % RING
            remote(e_v.at[RING * ty + tz, k], z_v.at[k, y, z], z_send.at[k], z_recv.at[k], (ty, x, tz, core)).start()
        pltpu.make_async_copy(e_v.at[RING * y + z, k], z_v.at[k, y, z], z_recv.at[k]).start()

    def two_levels(k, w, get, put):
        first = [pair_weight(w[b, 0, k], w[b + 1, 0, k]) for b in (0, 2)]
        second = [pair_weight(w[b, 1, k], w[b + 2, 1, k]) for b in (0, 1)]
        results = []
        for q in range(RING):
            b0, b1 = mix(first[0], get(0, q), get(1, q))
            b2, b3 = mix(first[1], get(2, q), get(3, q))
            results.append((b0, b1, b2, b3))
        for q, (b0, b1, b2, b3) in enumerate(results):
            b0, b2 = mix(second[0], b0, b2)
            b1, b3 = mix(second[1], b1, b3)
            results[q] = (b0, b1, b2, b3)
        for q in range(RING):
            for b in range(RING):
                put(b, q, results[q][b])

    def levels_z(k):
        pltpu.make_async_copy(z_v.at[k], z_v.at[k], z_recv.at[k]).wait()

        def put(b, q, value):
            z_v[k, q, b] = value

        two_levels(k, wz_v, lambda b, q: z_v[k, q, b], put)
        for d in (1, 3, 2):
            to = (x + d) % RING
            remote(z_v.at[k, :, to], x_v.at[k, x], x_send.at[k], x_recv.at[k], (y, to, z, core)).start()
        pltpu.make_async_copy(z_v.at[k, :, x], x_v.at[k, x], x_recv.at[k]).start()

    def levels_x(k):
        pltpu.make_async_copy(x_v.at[k], x_v.at[k], x_recv.at[k]).wait()

        def put(b, q, value):
            x_v[k, b, q] = value

        two_levels(k, wx_v, lambda b, q: x_v[k, b, q], put)
        for part in range(RING):
            rows = jnp.concatenate([x_v[k, :, q].reshape(RING * R2, COLS) for q in range(RING)], axis=1)
            total = dot(rows, table_v[:, pl.ds(part * COLS, COLS)])
            s_v[k, :, part] = total.astype(BF16).reshape(RING, R2, COLS)
        mine = RING * y + z
        for d in (5, 7, 13, 15, 1, 3, 4, 12, 6, 9, 11, 14, 2, 8, 10, 0):
            ty, tx = (y + d // RING) % RING, (x + d % RING) % RING

            def send_back(ty=ty, tx=tx):
                remote(s_v.at[k, tx, ty], out.at[mine, k], back_send.at[k], back_recv.at[k], (ty, tx, x, core)).start()

            if d == 0:
                pl.when(x != z)(send_back)

                @pl.when(x == z)
                def _():
                    pltpu.make_async_copy(s_v.at[k, x, y], out.at[mine, k], back_recv.at[k]).start()
            else:
                send_back()

    def step(t, carry):
        pl.when(t < CHUNKS)(lambda: level_6(t))
        pl.when((t >= 1) & (t < CHUNKS + 1))(lambda: level_7(t - 1))

        @pl.when(t == 2)
        def _():
            pltpu.make_async_copy(wz_v, wz_v, wz_recv).wait()

        pl.when((t >= 2) & (t < CHUNKS + 2))(lambda: levels_z(t - 2))

        @pl.when(t == 3)
        def _():
            pltpu.make_async_copy(wx_v, wx_v, wx_recv).wait()
            load_table.wait()

        pl.when(t >= 3)(lambda: levels_x(t - 3))
        return carry

    lax.fori_loop(0, CHUNKS + 3, step, 0)

    def finish(k, carry):
        send_core(k).wait_send()
        pltpu.make_async_copy(e_v.at[pl.ds(0, 15), k], e_v.at[pl.ds(0, 15), k], z_send.at[k]).wait()
        pltpu.make_async_copy(x_v.at[k, pl.ds(0, 3)], x_v.at[k, pl.ds(0, 3)], x_send.at[k]).wait()

        @pl.when(x != z)
        def _():
            pltpu.make_async_copy(s_v.at[k], s_v.at[k], back_send.at[k]).wait()

        @pl.when(x == z)
        def _():
            pltpu.make_async_copy(e_v.at[pl.ds(0, 15), k], e_v.at[pl.ds(0, 15), k], back_send.at[k]).wait()

        pltpu.make_async_copy(out.at[:, k], out.at[:, k], back_recv.at[k]).wait()
        return carry

    lax.fori_loop(0, CHUNKS, finish, 0)
    for held, sem in ((wy_v, wy_send), (wz_v, wz_send), (wx_v, wx_send)):
        pltpu.make_async_copy(held.at[pl.ds(0, 3)], held.at[pl.ds(0, 3)], sem).wait()


def model_kernel(basis, slow, out):
    def some(j, carry):
        rows = [
            lax.dot_general(basis[n], slow[n], (((0,), (0,)), ((), ())), preferred_element_type=F32).astype(BF16)
            for n in [j * BATCH + u for u in range(BATCH)]
        ]
        for u in range(BATCH):
            out[j * BATCH + u] = rows[u]
        return carry

    lax.fori_loop(0, basis.shape[0] // BATCH, some, 0)


def local(data, leaf_basis, level_weights, slowness_table, model_basis):
    any_space = pl.BlockSpec(memory_space=pl.ANY)
    levels = level_weights.shape[0]
    dma, vmem = pltpu.SemaphoreType.DMA, pltpu.VMEM
    slow = pl.pallas_call(
        main_kernel,
        out_shape=jax.ShapeDtypeStruct((GROUPS, CHUNKS, R2, COLS), BF16),
        in_specs=[any_space] * 4,
        out_specs=any_space,
        scratch_shapes=[
            vmem((GROUPS, CHUNKS, TB, COLS), BF16),
            vmem((GROUPS, CHUNKS, R2, TB), BF16),
            vmem((8, GROUPS, CHUNKS, R2, TB), BF16),
            vmem(slowness_table.shape, BF16),
            vmem((GROUPS, CHUNKS, R2, COLS), BF16),
            vmem((GROUPS, CHUNKS, R2, COLS), BF16),
            vmem((GROUPS, CHUNKS, R2, COLS), BF16),
            vmem((CHUNKS, RING, RING, R2, COLS), BF16),
            vmem((CHUNKS, RING, RING, R2, COLS), BF16),
            vmem((CHUNKS, RING, RING, R2, COLS), BF16),
            vmem((RING, 2, CHUNKS, R2, TB), BF16),
            vmem((RING, 2, CHUNKS, R2, TB), BF16),
            vmem((RING, 2, CHUNKS, R2, TB), BF16),
            dma((CHUNKS,)), dma((CHUNKS,)), dma((8,)), dma,
            dma, dma, dma, dma, dma, dma,
            dma((CHUNKS,)), dma((CHUNKS,)), dma((CHUNKS,)), dma((CHUNKS,)),
            dma((CHUNKS,)), dma((CHUNKS,)), dma((CHUNKS,)), dma((CHUNKS,)),
        ],
        compiler_params=pltpu.CompilerParams(collective_id=0, has_side_effects=True, vmem_limit_bytes=58 << 20),
    )(
        data.reshape(GROUPS, CHUNKS, TB, COLS),
        leaf_basis.reshape(GROUPS, CHUNKS, R2, TB),
        level_weights.reshape(levels, GROUPS, CHUNKS, R2, TB),
        slowness_table,
    )
    blocks = GROUPS * CHUNKS
    step = 16
    model = pl.pallas_call(
        model_kernel,
        grid=(blocks // step,),
        out_shape=jax.ShapeDtypeStruct((blocks, TB, COLS), BF16),
        in_specs=[
            pl.BlockSpec((step, R2, TB), lambda n: (n, 0, 0)),
            pl.BlockSpec((step, R2, COLS), lambda n: (n, 0, 0)),
        ],
        out_specs=pl.BlockSpec((step, TB, COLS), lambda n: (n, 0, 0)),
        compiler_params=pltpu.CompilerParams(vmem_limit_bytes=58 << 20),
    )(model_basis, slow.reshape(blocks, R2, COLS))
    return model.reshape(blocks * TB, COLS)


def solution(mesh):
    placed = (
        P("tm", "off"),
        P("tm", None, None),
        P(None, "tm", None, None),
        P(),
        P("tm", None, None),
    )
    return jax.shard_map(local, mesh=mesh, in_specs=placed, out_specs=P("tm", "off"), check_vma=False)
```

```python
import functools

import jax
import jax.numpy as jnp
from jax import lax
from jax.experimental import pallas as pl
from jax.experimental.pallas import tpu as pltpu
from jax.sharding import PartitionSpec as P

MESH = pl.DeviceIdType.MESH
F32, BF16 = jnp.float32, jnp.bfloat16
CHUNKS = 8
RING = 4
GROUPS = RING * RING
BATCH = 16
R2, TB, COLS = 64, 128, 256
HALF = COLS // 2


def place():
    y, tm = lax.axis_index("off"), lax.axis_index("tm")
    return y, tm // 8, (tm // 2) % 4, tm % 2


def device(y, x, z, core):
    return (y, x * 8 + z * 2 + core)


def dot(a, b):
    return jnp.dot(a, b, preferred_element_type=F32)


def pair_weight(own, partner):
    swapped = jnp.concatenate([partner[:, R2:], partner[:, :R2]], axis=1)
    return jnp.concatenate([own, swapped], axis=0)


def mix(weight, low, high):
    out = dot(weight, jnp.concatenate([low, high], axis=0)).astype(BF16)
    return out[:R2], out[R2:]


def tell_all(y, x, z, core):
    barrier = pltpu.get_barrier_semaphore()

    def tell(*there):
        pl.semaphore_signal(barrier, inc=1, device_id=device(*there), device_id_type=MESH)

    tell(y, x, z, 1 - core)
    for d in range(1, GROUPS):
        tell((y + d // RING) % RING, x, (z + d % RING) % RING, core)
    for d in range(1, RING):
        tell(y, (x + d) % RING, z, core)
    for dy in range(RING):
        for d in range(RING):
            source_z = (z + d) % RING
            if dy == 0 and d == 0:
                continue
            pl.when(x != z)(functools.partial(tell, (y + dy) % RING, z, source_z, core))
        for d in range(1, RING):
            there = (x + d) % RING
            new = (x != z) & (there != z)
            if dy > 0:
                new = new | (x == z)
            pl.when(new)(functools.partial(tell, (y + dy) % RING, there, x, core))


def main_kernel(
    data, leaf, weights, table, out,
    data_v, leaf_v, w_v, table_v, c_v, sib_v, e_v, z_v, x_v, s_v, wy_v, wz_v, wx_v,
    data_sem, leaf_sem, w_sem, table_sem, wy_send, wy_recv, wz_send, wz_recv, wx_send, wx_recv,
    core_send, core_recv, z_send, z_recv, x_send, x_recv, back_send, back_recv,
):
    y, x, z, core = place()
    per = GROUPS // CHUNKS

    def load_data(p):
        return pltpu.make_async_copy(data.at[pl.ds(p * per, per)], data_v.at[pl.ds(p * per, per)], data_sem.at[p])

    def load_leaf(p):
        return pltpu.make_async_copy(leaf.at[pl.ds(p * per, per)], leaf_v.at[pl.ds(p * per, per)], leaf_sem.at[p])

    def load_w(level):
        return pltpu.make_async_copy(weights.at[level], w_v.at[level], w_sem.at[level])

    for p in range(CHUNKS):
        load_leaf(p).start()
        load_data(p).start()
    for level in range(8):
        load_w(level).start()
    for half in range(2):
        for q in range(RING):
            rows = table.at[pl.ds(q * COLS + half * HALF, HALF)]
            pltpu.make_async_copy(rows, table_v.at[pl.ds((half * RING + q) * HALF, HALF)], table_sem).start()

    tell_all(y, x, z, core)

    def remote(src, dst, send, recv, there):
        return pltpu.make_async_remote_copy(
            src_ref=src, dst_ref=dst, send_sem=send, recv_sem=recv, device_id=device(*there), device_id_type=MESH
        )

    def leaf_part(p, carry):
        load_leaf(p).wait()
        load_data(p).wait()

        def some(j, carry):
            a = p * per + j
            parts = [dot(leaf_v[a, k], data_v[a, k]).astype(BF16) for k in range(CHUNKS)]
            for k in range(CHUNKS):
                c_v[a, k] = parts[k]
            return carry

        return lax.fori_loop(0, per, some, carry)

    lax.fori_loop(0, 2, leaf_part, 0)
    pl.semaphore_wait(pltpu.get_barrier_semaphore(), jnp.where(x == z, 28, 42))

    for first, dst, send, recv in ((10, wy_v, wy_send, wy_recv), (8, wz_v, wz_send, wz_recv)):
        for d in (1, 3, 2):
            to = (z + d) % RING
            remote(weights.at[pl.ds(first, 2), RING * y + to], dst.at[z], send, recv, (y, x, to, core)).start()
        pltpu.make_async_copy(weights.at[pl.ds(first, 2), RING * y + z], dst.at[z], recv).start()
    lax.fori_loop(2, CHUNKS, leaf_part, 0)

    def forward_weights():
        pltpu.make_async_copy(wy_v, wy_v, wy_recv).wait()
        for d in (1, 3, 2):
            to = (x + d) % RING
            remote(wy_v.at[to], wx_v.at[x], wx_send, wx_recv, (y, to, z, core)).start()
        pltpu.make_async_copy(wy_v.at[x], wx_v.at[x], wx_recv).start()

    def mix_blocks(level, pairs):
        mixed = [
            mix(pair_weight(w_v[(level, *low)], w_v[(level, *high)]), c_v[low], c_v[high]) for low, high in pairs
        ]
        for (low, high), (first, second) in zip(pairs, mixed):
            c_v[low], c_v[high] = first, second

    for level in range(6):
        load_w(level).wait()
        spacing = 2**level

        def some(j, carry, level=level, spacing=spacing):
            pairs = []
            for u in range(BATCH):
                n = j * BATCH + u
                low = (n // spacing) * (2 * spacing) + n % spacing
                high = low + spacing
                pairs.append(((low // CHUNKS, low % CHUNKS), (high // CHUNKS, high % CHUNKS)))
            mix_blocks(level, pairs)
            return carry

        lax.fori_loop(0, GROUPS * CHUNKS // 2 // BATCH, some, 0)
    load_w(6).wait()
    load_w(7).wait()
    forward_weights()

    def send_core(k):
        return remote(c_v.at[:, k], sib_v.at[:, k], core_send.at[k], core_recv.at[k], (y, x, z, 1 - core))

    def level_6(k):
        mix_blocks(6, [((a, k), (a + GROUPS // 2, k)) for a in range(GROUPS // 2)])
        send_core(k).start()

    def level_7(k):
        send_core(k).wait_recv()

        mixed = [
            dot(w_v[7, a, k], jnp.concatenate([c_v[a, k], sib_v[a, k]], axis=0)).astype(BF16) for a in range(GROUPS)
        ]
        for a in range(GROUPS):
            e_v[a, k] = mixed[a]

    def send_z(k, half):
        part = pl.ds(half * HALF, HALF)
        there = pl.ds(pl.multiple_of(y * HALF, HALF), HALF)
        for d in (5, 7, 13, 15, 1, 3, 4, 12, 6, 9, 11, 14, 2, 8, 10):
            ty, tz = (y + d // RING) % RING, (z + d % RING) % RING
            remote(
                e_v.at[RING * ty + tz, k, :, part], z_v.at[k, half, z, :, there],
                z_send.at[k, half], z_recv.at[k, half], (ty, x, tz, core),
            ).start()
        mine = e_v.at[RING * y + z, k, :, part]
        pltpu.make_async_copy(mine, z_v.at[k, half, z, :, there], z_recv.at[k, half]).start()

    def two_levels(k, w, held):
        first = [pair_weight(w[b, 0, k], w[b + 1, 0, k]) for b in (0, 2)]
        second = [pair_weight(w[b, 1, k], w[b + 2, 1, k]) for b in (0, 1)]
        b0, b1 = mix(first[0], held[0], held[1])
        b2, b3 = mix(first[1], held[2], held[3])
        b0, b2 = mix(second[0], b0, b2)
        b1, b3 = mix(second[1], b1, b3)
        for b, value in enumerate((b0, b1, b2, b3)):
            held[b] = value

    def levels_z(k, half):
        held = z_v.at[k, half]
        pltpu.make_async_copy(held, held, z_recv.at[k, half]).wait()
        two_levels(k, wz_v, held)
        for d in (1, 3, 2):
            to = (x + d) % RING
            remote(held.at[to], x_v.at[k, half, x], x_send.at[k, half], x_recv.at[k, half], (y, to, z, core)).start()
        pltpu.make_async_copy(held.at[x], x_v.at[k, half, x], x_recv.at[k, half]).start()

    def levels_x(k, half):
        held = x_v.at[k, half]
        pltpu.make_async_copy(held, held, x_recv.at[k, half]).wait()
        two_levels(k, wx_v, held)

    def slowness(k):
        mine = RING * y + z
        rows = jnp.concatenate([x_v[k, half].reshape(RING * R2, RING * HALF) for half in range(2)], axis=1)
        for dy in (1, 3, 2, 0):
            part = (y + dy) % RING
            total = dot(rows, table_v[:, pl.ds(pl.multiple_of(part * COLS, COLS), COLS)])
            s_v[k, :, part] = total.astype(BF16).reshape(RING, R2, COLS)
            for d in (1, 3, 2, 0):
                tx = (x + d) % RING

                def send_back(tx=tx):
                    remote(s_v.at[k, tx, part], out.at[mine, k], back_send.at[k], back_recv.at[k], (part, tx, x, core)).start()

                if d == 0 and dy == 0:
                    pl.when(x != z)(send_back)

                    @pl.when(x == z)
                    def _():
                        pltpu.make_async_copy(s_v.at[k, x, part], out.at[mine, k], back_recv.at[k]).start()
                else:
                    send_back()

    def step(t, carry):
        now, before, last = t < CHUNKS, (t >= 2) & (t < CHUNKS + 2), t >= 3

        pl.when(now)(lambda: level_6(t))

        @pl.when((t >= 1) & (t < CHUNKS + 1))
        def _():
            level_7(t - 1)
            send_z(t - 1, 0)

        @pl.when(t == 2)
        def _():
            pltpu.make_async_copy(wz_v, wz_v, wz_recv).wait()

        pl.when(before)(lambda: levels_z(t - 2, 0))
        pl.when((t >= 1) & (t < CHUNKS + 1))(lambda: send_z(t - 1, 1))

        @pl.when(last)
        def _():
            levels_x(t - 3, 1)
            slowness(t - 3)

        pl.when(before)(lambda: levels_z(t - 2, 1))

        @pl.when(t == 2)
        def _():
            pltpu.make_async_copy(wx_v, wx_v, wx_recv).wait()
            pltpu.make_async_copy(table_v, table_v, table_sem).wait()

        pl.when(before)(lambda: levels_x(t - 2, 0))
        return carry

    lax.fori_loop(0, CHUNKS + 3, step, 0)

    def finish(k, carry):
        send_core(k).wait_send()
        for half in range(2):
            sent = e_v.at[pl.ds(0, 15), k, :, pl.ds(half * HALF, HALF)]
            pltpu.make_async_copy(sent, sent, z_send.at[k, half]).wait()
            sent = x_v.at[k, half, pl.ds(0, 3)]
            pltpu.make_async_copy(sent, sent, x_send.at[k, half]).wait()

        @pl.when(x != z)
        def _():
            pltpu.make_async_copy(s_v.at[k], s_v.at[k], back_send.at[k]).wait()

        @pl.when(x == z)
        def _():
            pltpu.make_async_copy(e_v.at[pl.ds(0, 15), k], e_v.at[pl.ds(0, 15), k], back_send.at[k]).wait()

        pltpu.make_async_copy(out.at[:, k], out.at[:, k], back_recv.at[k]).wait()
        return carry

    lax.fori_loop(0, CHUNKS, finish, 0)
    for held, sem in ((wy_v, wy_send), (wz_v, wz_send), (wx_v, wx_send)):
        pltpu.make_async_copy(held.at[pl.ds(0, 3)], held.at[pl.ds(0, 3)], sem).wait()


def model_kernel(basis, slow, out):
    def some(j, carry):
        rows = [
            lax.dot_general(basis[n], slow[n], (((0,), (0,)), ((), ())), preferred_element_type=F32).astype(BF16)
            for n in [j * BATCH + u for u in range(BATCH)]
        ]
        for u in range(BATCH):
            out[j * BATCH + u] = rows[u]
        return carry

    lax.fori_loop(0, basis.shape[0] // BATCH, some, 0)


def local(data, leaf_basis, level_weights, slowness_table, model_basis):
    any_space = pl.BlockSpec(memory_space=pl.ANY)
    levels = level_weights.shape[0]
    dma, vmem = pltpu.SemaphoreType.DMA, pltpu.VMEM
    slow = pl.pallas_call(
        main_kernel,
        out_shape=jax.ShapeDtypeStruct((GROUPS, CHUNKS, R2, COLS), BF16),
        in_specs=[any_space] * 4,
        out_specs=any_space,
        scratch_shapes=[
            vmem((GROUPS, CHUNKS, TB, COLS), BF16),
            vmem((GROUPS, CHUNKS, R2, TB), BF16),
            vmem((8, GROUPS, CHUNKS, R2, TB), BF16),
            vmem(slowness_table.shape, BF16),
            vmem((GROUPS, CHUNKS, R2, COLS), BF16),
            vmem((GROUPS, CHUNKS, R2, COLS), BF16),
            vmem((GROUPS, CHUNKS, R2, COLS), BF16),
            vmem((CHUNKS, 2, RING, R2, RING * HALF), BF16),
            vmem((CHUNKS, 2, RING, R2, RING * HALF), BF16),
            vmem((CHUNKS, RING, RING, R2, COLS), BF16),
            vmem((RING, 2, CHUNKS, R2, TB), BF16),
            vmem((RING, 2, CHUNKS, R2, TB), BF16),
            vmem((RING, 2, CHUNKS, R2, TB), BF16),
            dma((CHUNKS,)), dma((CHUNKS,)), dma((8,)), dma,
            dma, dma, dma, dma, dma, dma,
            dma((CHUNKS,)), dma((CHUNKS,)), dma((CHUNKS, 2)), dma((CHUNKS, 2)),
            dma((CHUNKS, 2)), dma((CHUNKS, 2)), dma((CHUNKS,)), dma((CHUNKS,)),
        ],
        compiler_params=pltpu.CompilerParams(collective_id=0, has_side_effects=True, vmem_limit_bytes=58 << 20),
    )(
        data.reshape(GROUPS, CHUNKS, TB, COLS),
        leaf_basis.reshape(GROUPS, CHUNKS, R2, TB),
        level_weights.reshape(levels, GROUPS, CHUNKS, R2, TB),
        slowness_table,
    )
    blocks = GROUPS * CHUNKS
    step = 32
    model = pl.pallas_call(
        model_kernel,
        grid=(blocks // step,),
        out_shape=jax.ShapeDtypeStruct((blocks, TB, COLS), BF16),
        in_specs=[
            pl.BlockSpec((step, R2, TB), lambda n: (n, 0, 0)),
            pl.BlockSpec((step, R2, COLS), lambda n: (n, 0, 0)),
        ],
        out_specs=pl.BlockSpec((step, TB, COLS), lambda n: (n, 0, 0)),
        compiler_params=pltpu.CompilerParams(vmem_limit_bytes=58 << 20),
    )(model_basis, slow.reshape(blocks, R2, COLS))
    return model.reshape(blocks * TB, COLS)


def solution(mesh):
    placed = (
        P("tm", "off"),
        P("tm", None, None),
        P(None, "tm", None, None),
        P(),
        P("tm", None, None),
    )
    return jax.shard_map(local, mesh=mesh, in_specs=placed, out_specs=P("tm", "off"), check_vma=False)
```

```python
import functools

import jax
import jax.numpy as jnp
from jax import lax
from jax.experimental import pallas as pl
from jax.experimental.pallas import tpu as pltpu
from jax.sharding import PartitionSpec as P

MESH = pl.DeviceIdType.MESH
F32, BF16 = jnp.float32, jnp.bfloat16
CHUNKS = 8
RING = 4
GROUPS = RING * RING
BATCH = 16
PIECE = 32
R2, TB, COLS = 64, 128, 256
HALF = COLS // 2


def place():
    y, tm = lax.axis_index("off"), lax.axis_index("tm")
    return y, tm // 8, (tm // 2) % 4, tm % 2


def device(y, x, z, core):
    return (y, x * 8 + z * 2 + core)


def dot(a, b):
    return jnp.dot(a, b, preferred_element_type=F32)


def pair_weight(own, partner):
    swapped = jnp.concatenate([partner[:, R2:], partner[:, :R2]], axis=1)
    return jnp.concatenate([own, swapped], axis=0)


def mix(weight, low, high):
    out = dot(weight, jnp.concatenate([low, high], axis=0)).astype(BF16)
    return out[:R2], out[R2:]


def tell_all(y, x, z, core):
    barrier = pltpu.get_barrier_semaphore()

    def tell(*there):
        pl.semaphore_signal(barrier, inc=1, device_id=device(*there), device_id_type=MESH)

    tell(y, x, z, 1 - core)
    for d in range(1, GROUPS):
        tell((y + d // RING) % RING, x, (z + d % RING) % RING, core)
    for d in range(1, RING):
        tell(y, (x + d) % RING, z, core)
    for dy in range(RING):
        for d in range(RING):
            source_z = (z + d) % RING
            if dy == 0 and d == 0:
                continue
            pl.when(x != z)(functools.partial(tell, (y + dy) % RING, z, source_z, core))
        for d in range(1, RING):
            there = (x + d) % RING
            new = (x != z) & (there != z)
            if dy > 0:
                new = new | (x == z)
            pl.when(new)(functools.partial(tell, (y + dy) % RING, there, x, core))


def main_kernel(
    data, leaf, weights, table, out,
    data_v, leaf_v, w_v, table_v, c_v, sib_v, e_v, z_v, x_v, s_v, wy_v, wz_v, wx_v,
    data_sem, leaf_sem, w_sem, table_sem, wy_send, wy_recv, wz_send, wz_recv, wx_send, wx_recv,
    core_send, core_recv, z_send, z_recv, x_send, x_recv, back_send, back_recv,
):
    y, x, z, core = place()
    per = GROUPS // CHUNKS

    def load_data(p):
        return pltpu.make_async_copy(data.at[pl.ds(p * per, per)], data_v.at[pl.ds(p * per, per)], data_sem.at[p])

    def load_leaf(p):
        return pltpu.make_async_copy(leaf.at[pl.ds(p * per, per)], leaf_v.at[pl.ds(p * per, per)], leaf_sem.at[p])

    def load_w(level):
        return pltpu.make_async_copy(weights.at[level], w_v.at[level], w_sem.at[level])

    for p in range(CHUNKS):
        load_leaf(p).start()
        load_data(p).start()
    for level in range(8):
        load_w(level).start()
    for half in range(2):
        for q in range(RING):
            rows = table.at[pl.ds(q * COLS + half * HALF, HALF)]
            pltpu.make_async_copy(rows, table_v.at[pl.ds((half * RING + q) * HALF, HALF)], table_sem).start()

    tell_all(y, x, z, core)

    def remote(src, dst, send, recv, there):
        return pltpu.make_async_remote_copy(
            src_ref=src, dst_ref=dst, send_sem=send, recv_sem=recv, device_id=device(*there), device_id_type=MESH
        )

    def leaf_part(p, carry):
        load_leaf(p).wait()
        load_data(p).wait()

        def some(j, carry):
            a = p * per + j
            parts = [dot(leaf_v[a, k], data_v[a, k]).astype(BF16) for k in range(CHUNKS)]
            for k in range(CHUNKS):
                c_v[a, k] = parts[k]
            return carry

        return lax.fori_loop(0, per, some, carry)

    lax.fori_loop(0, 2, leaf_part, 0)
    pl.semaphore_wait(pltpu.get_barrier_semaphore(), jnp.where(x == z, 28, 42))

    for first, dst, send, recv in ((10, wy_v, wy_send, wy_recv), (8, wz_v, wz_send, wz_recv)):
        for d in (1, 3, 2):
            to = (z + d) % RING
            remote(weights.at[pl.ds(first, 2), RING * y + to], dst.at[z], send, recv, (y, x, to, core)).start()
        pltpu.make_async_copy(weights.at[pl.ds(first, 2), RING * y + z], dst.at[z], recv).start()
    lax.fori_loop(2, CHUNKS, leaf_part, 0)

    def forward_weights():
        pltpu.make_async_copy(wy_v, wy_v, wy_recv).wait()
        for d in (1, 3, 2):
            to = (x + d) % RING
            remote(wy_v.at[to], wx_v.at[x], wx_send, wx_recv, (y, to, z, core)).start()
        pltpu.make_async_copy(wy_v.at[x], wx_v.at[x], wx_recv).start()

    def mix_blocks(level, pairs):
        mixed = [
            mix(pair_weight(w_v[(level, *low)], w_v[(level, *high)]), c_v[low], c_v[high]) for low, high in pairs
        ]
        for (low, high), (first, second) in zip(pairs, mixed):
            c_v[low], c_v[high] = first, second

    for level in range(6):
        load_w(level).wait()
        spacing = 2**level

        def some(j, carry, level=level, spacing=spacing):
            pairs = []
            for u in range(BATCH):
                n = j * BATCH + u
                low = (n // spacing) * (2 * spacing) + n % spacing
                high = low + spacing
                pairs.append(((low // CHUNKS, low % CHUNKS), (high // CHUNKS, high % CHUNKS)))
            mix_blocks(level, pairs)
            return carry

        lax.fori_loop(0, GROUPS * CHUNKS // 2 // BATCH, some, 0)
    load_w(6).wait()
    load_w(7).wait()
    forward_weights()

    def send_core(k):
        return remote(c_v.at[:, k], sib_v.at[:, k], core_send.at[k], core_recv.at[k], (y, x, z, 1 - core))

    def level_6(k):
        mix_blocks(6, [((a, k), (a + GROUPS // 2, k)) for a in range(GROUPS // 2)])
        send_core(k).start()

    def level_7(k):
        send_core(k).wait_recv()

        mixed = [
            dot(w_v[7, a, k], jnp.concatenate([c_v[a, k], sib_v[a, k]], axis=0)).astype(BF16) for a in range(GROUPS)
        ]
        for a in range(GROUPS):
            e_v[a, k] = mixed[a]

    def send_z(k, half):
        part = pl.ds(half * HALF, HALF)
        there = pl.ds(pl.multiple_of(y * HALF, HALF), HALF)
        for d in (5, 7, 13, 15, 1, 3, 4, 12, 6, 9, 11, 14, 2, 8, 10):
            ty, tz = (y + d // RING) % RING, (z + d % RING) % RING
            remote(
                e_v.at[RING * ty + tz, k, :, part], z_v.at[k, half, z, :, there],
                z_send.at[k, half], z_recv.at[k, half], (ty, x, tz, core),
            ).start()
        mine = e_v.at[RING * y + z, k, :, part]
        pltpu.make_async_copy(mine, z_v.at[k, half, z, :, there], z_recv.at[k, half]).start()

    def two_levels(k, w, held):
        first = [pair_weight(w[b, 0, k], w[b + 1, 0, k]) for b in (0, 2)]
        second = [pair_weight(w[b, 1, k], w[b + 2, 1, k]) for b in (0, 1)]
        b0, b1 = mix(first[0], held[0], held[1])
        b2, b3 = mix(first[1], held[2], held[3])
        b0, b2 = mix(second[0], b0, b2)
        b1, b3 = mix(second[1], b1, b3)
        for b, value in enumerate((b0, b1, b2, b3)):
            held[b] = value

    def levels_z(k, half):
        held = z_v.at[k, half]
        pltpu.make_async_copy(held, held, z_recv.at[k, half]).wait()
        two_levels(k, wz_v, held)
        for d in (1, 3, 2):
            to = (x + d) % RING
            remote(held.at[to], x_v.at[k, half, x], x_send.at[k, half], x_recv.at[k, half], (y, to, z, core)).start()
        pltpu.make_async_copy(held.at[x], x_v.at[k, half, x], x_recv.at[k, half]).start()

    def levels_x(k, half):
        held = x_v.at[k, half]
        pltpu.make_async_copy(held, held, x_recv.at[k, half]).wait()
        two_levels(k, wx_v, held)

    def slowness(k):
        mine = RING * y + z
        rows = jnp.concatenate([x_v[k, half].reshape(RING * R2, RING * HALF) for half in range(2)], axis=1)
        for dy in (1, 3, 2, 0):
            part = (y + dy) % RING
            total = dot(rows, table_v[:, pl.ds(pl.multiple_of(part * COLS, COLS), COLS)])
            s_v[k, :, part] = total.astype(BF16).reshape(RING, R2, COLS)
            for d in (1, 3, 2, 0):
                tx = (x + d) % RING

                def send_back(tx=tx):
                    remote(s_v.at[k, tx, part], out.at[mine, k], back_send.at[k], back_recv.at[k], (part, tx, x, core)).start()

                if d == 0 and dy == 0:
                    pl.when(x != z)(send_back)

                    @pl.when(x == z)
                    def _():
                        pltpu.make_async_copy(s_v.at[k, x, part], out.at[mine, k], back_recv.at[k]).start()
                else:
                    send_back()

    def step(t, carry):
        now, before, last = t < CHUNKS, (t >= 2) & (t < CHUNKS + 2), t >= 3

        pl.when(now)(lambda: level_6(t))

        @pl.when((t >= 1) & (t < CHUNKS + 1))
        def _():
            level_7(t - 1)
            send_z(t - 1, 0)

        @pl.when(t == 2)
        def _():
            pltpu.make_async_copy(wz_v, wz_v, wz_recv).wait()

        pl.when(before)(lambda: levels_z(t - 2, 0))
        pl.when((t >= 1) & (t < CHUNKS + 1))(lambda: send_z(t - 1, 1))

        @pl.when(last)
        def _():
            levels_x(t - 3, 1)
            slowness(t - 3)

        pl.when(before)(lambda: levels_z(t - 2, 1))

        @pl.when(t == 2)
        def _():
            pltpu.make_async_copy(wx_v, wx_v, wx_recv).wait()
            pltpu.make_async_copy(table_v, table_v, table_sem).wait()

        pl.when(before)(lambda: levels_x(t - 2, 0))
        return carry

    lax.fori_loop(0, CHUNKS + 3, step, 0)

    def finish(k, carry):
        send_core(k).wait_send()
        for half in range(2):
            sent = e_v.at[pl.ds(0, 15), k, :, pl.ds(half * HALF, HALF)]
            pltpu.make_async_copy(sent, sent, z_send.at[k, half]).wait()
            sent = x_v.at[k, half, pl.ds(0, 3)]
            pltpu.make_async_copy(sent, sent, x_send.at[k, half]).wait()

        @pl.when(x != z)
        def _():
            pltpu.make_async_copy(s_v.at[k], s_v.at[k], back_send.at[k]).wait()

        @pl.when(x == z)
        def _():
            pltpu.make_async_copy(e_v.at[pl.ds(0, 15), k], e_v.at[pl.ds(0, 15), k], back_send.at[k]).wait()

        pltpu.make_async_copy(out.at[:, k], out.at[:, k], back_recv.at[k]).wait()
        return carry

    lax.fori_loop(0, CHUNKS, finish, 0)
    for held, sem in ((wy_v, wy_send), (wz_v, wz_send), (wx_v, wx_send)):
        pltpu.make_async_copy(held.at[pl.ds(0, 3)], held.at[pl.ds(0, 3)], sem).wait()


def model_kernel(basis, slow, out, basis_v, slow_v, out_v, basis_sem, slow_sem, out_sem):
    def piece(ref, p):
        return ref.at[pl.ds(p * PIECE, PIECE)]

    def load(p):
        return (
            pltpu.make_async_copy(piece(basis, p), piece(basis_v, p), basis_sem.at[p]),
            pltpu.make_async_copy(piece(slow, p), piece(slow_v, p), slow_sem.at[p]),
        )

    def store(p):
        return pltpu.make_async_copy(piece(out_v, p), piece(out, p), out_sem.at[p])

    pieces = basis.shape[0] // PIECE
    for p in range(pieces):
        for copy in load(p):
            copy.start()

    def some(p, carry):
        for copy in load(p):
            copy.wait()
        at = [p * PIECE + u for u in range(PIECE)]
        rows = [
            lax.dot_general(basis_v[n], slow_v[n], (((0,), (0,)), ((), ())), preferred_element_type=F32).astype(BF16)
            for n in at
        ]
        for u in range(PIECE):
            out_v[at[u]] = rows[u]
        store(p).start()
        return carry

    lax.fori_loop(0, pieces, some, 0)

    def finish(p, carry):
        store(p).wait()
        return carry

    lax.fori_loop(0, pieces, finish, 0)


def local(data, leaf_basis, level_weights, slowness_table, model_basis):
    any_space = pl.BlockSpec(memory_space=pl.ANY)
    levels = level_weights.shape[0]
    dma, vmem = pltpu.SemaphoreType.DMA, pltpu.VMEM
    slow = pl.pallas_call(
        main_kernel,
        out_shape=jax.ShapeDtypeStruct((GROUPS, CHUNKS, R2, COLS), BF16),
        in_specs=[any_space] * 4,
        out_specs=any_space,
        scratch_shapes=[
            vmem((GROUPS, CHUNKS, TB, COLS), BF16),
            vmem((GROUPS, CHUNKS, R2, TB), BF16),
            vmem((8, GROUPS, CHUNKS, R2, TB), BF16),
            vmem(slowness_table.shape, BF16),
            vmem((GROUPS, CHUNKS, R2, COLS), BF16),
            vmem((GROUPS, CHUNKS, R2, COLS), BF16),
            vmem((GROUPS, CHUNKS, R2, COLS), BF16),
            vmem((CHUNKS, 2, RING, R2, RING * HALF), BF16),
            vmem((CHUNKS, 2, RING, R2, RING * HALF), BF16),
            vmem((CHUNKS, RING, RING, R2, COLS), BF16),
            vmem((RING, 2, CHUNKS, R2, TB), BF16),
            vmem((RING, 2, CHUNKS, R2, TB), BF16),
            vmem((RING, 2, CHUNKS, R2, TB), BF16),
            dma((CHUNKS,)), dma((CHUNKS,)), dma((8,)), dma,
            dma, dma, dma, dma, dma, dma,
            dma((CHUNKS,)), dma((CHUNKS,)), dma((CHUNKS, 2)), dma((CHUNKS, 2)),
            dma((CHUNKS, 2)), dma((CHUNKS, 2)), dma((CHUNKS,)), dma((CHUNKS,)),
        ],
        compiler_params=pltpu.CompilerParams(collective_id=0, has_side_effects=True, vmem_limit_bytes=58 << 20),
    )(
        data.reshape(GROUPS, CHUNKS, TB, COLS),
        leaf_basis.reshape(GROUPS, CHUNKS, R2, TB),
        level_weights.reshape(levels, GROUPS, CHUNKS, R2, TB),
        slowness_table,
    )
    blocks = GROUPS * CHUNKS
    pieces = blocks // PIECE
    model = pl.pallas_call(
        model_kernel,
        out_shape=jax.ShapeDtypeStruct((blocks, TB, COLS), BF16),
        in_specs=[any_space] * 2,
        out_specs=any_space,
        scratch_shapes=[
            vmem((blocks, R2, TB), BF16), vmem((blocks, R2, COLS), BF16), vmem((blocks, TB, COLS), BF16),
            dma((pieces,)), dma((pieces,)), dma((pieces,)),
        ],
        compiler_params=pltpu.CompilerParams(vmem_limit_bytes=58 << 20),
    )(model_basis, slow.reshape(blocks, R2, COLS))
    return model.reshape(blocks * TB, COLS)


def solution(mesh):
    placed = (
        P("tm", "off"),
        P("tm", None, None),
        P(None, "tm", None, None),
        P(),
        P("tm", None, None),
    )
    return jax.shard_map(local, mesh=mesh, in_specs=placed, out_specs=P("tm", "off"), check_vma=False)
```

```python
import functools

import jax
import jax.numpy as jnp
from jax import lax
from jax.experimental import pallas as pl
from jax.experimental.pallas import tpu as pltpu
from jax.sharding import PartitionSpec as P

MESH = pl.DeviceIdType.MESH
F32, BF16 = jnp.float32, jnp.bfloat16
CHUNKS = 8
RING = 4
GROUPS = RING * RING
BATCH = 16
PIECE = 32
R2, TB, COLS = 64, 128, 256
HALF = COLS // 2


def place():
    y, tm = lax.axis_index("off"), lax.axis_index("tm")
    return y, tm // 8, (tm // 2) % 4, tm % 2


def device(y, x, z, core):
    return (y, x * 8 + z * 2 + core)


def dot(a, b):
    return jnp.dot(a, b, preferred_element_type=F32)


def pair_weight(own, partner):
    swapped = jnp.concatenate([partner[:, R2:], partner[:, :R2]], axis=1)
    return jnp.concatenate([own, swapped], axis=0)


def mix(weight, low, high):
    out = dot(weight, jnp.concatenate([low, high], axis=0)).astype(BF16)
    return out[:R2], out[R2:]


def tell_all(y, x, z, core):
    barrier = pltpu.get_barrier_semaphore()

    def tell(*there):
        pl.semaphore_signal(barrier, inc=1, device_id=device(*there), device_id_type=MESH)

    tell(y, x, z, 1 - core)
    for d in range(1, GROUPS):
        tell((y + d // RING) % RING, x, (z + d % RING) % RING, core)
    for d in range(1, RING):
        tell(y, (x + d) % RING, z, core)
    for dy in range(RING):
        for d in range(RING):
            source_z = (z + d) % RING
            if dy == 0 and d == 0:
                continue
            pl.when(x != z)(functools.partial(tell, (y + dy) % RING, z, source_z, core))
        for d in range(1, RING):
            there = (x + d) % RING
            new = (x != z) & (there != z)
            if dy > 0:
                new = new | (x == z)
            pl.when(new)(functools.partial(tell, (y + dy) % RING, there, x, core))


def main_kernel(
    data, leaf, weights, table, out,
    data_v, leaf_v, w_v, table_v, c_v, sib_v, e_v, z_v, x_v, s_v, wy_v, wz_v, wx_v,
    data_sem, leaf_sem, w_sem, table_sem, wy_send, wy_recv, wz_send, wz_recv, wx_send, wx_recv,
    core_send, core_recv, z_send, z_recv, x_send, x_recv, back_send, back_recv,
):
    y, x, z, core = place()
    turn = 1 + 2 * core
    per = GROUPS // CHUNKS

    def load_data(p):
        return pltpu.make_async_copy(data.at[pl.ds(p * per, per)], data_v.at[pl.ds(p * per, per)], data_sem.at[p])

    def load_leaf(p):
        return pltpu.make_async_copy(leaf.at[pl.ds(p * per, per)], leaf_v.at[pl.ds(p * per, per)], leaf_sem.at[p])

    def load_w(level):
        return pltpu.make_async_copy(weights.at[level], w_v.at[level], w_sem.at[level])

    for p in range(CHUNKS):
        load_leaf(p).start()
        load_data(p).start()
    for level in range(8):
        load_w(level).start()
    for half in range(2):
        for q in range(RING):
            rows = table.at[pl.ds(q * COLS + half * HALF, HALF)]
            pltpu.make_async_copy(rows, table_v.at[pl.ds((half * RING + q) * HALF, HALF)], table_sem).start()

    tell_all(y, x, z, core)

    def remote(src, dst, send, recv, there):
        return pltpu.make_async_remote_copy(
            src_ref=src, dst_ref=dst, send_sem=send, recv_sem=recv, device_id=device(*there), device_id_type=MESH
        )

    def leaf_part(p, carry):
        load_leaf(p).wait()
        load_data(p).wait()

        def some(j, carry):
            a = p * per + j
            parts = [dot(leaf_v[a, k], data_v[a, k]).astype(BF16) for k in range(CHUNKS)]
            for k in range(CHUNKS):
                c_v[a, k] = parts[k]
            return carry

        return lax.fori_loop(0, per, some, carry)

    lax.fori_loop(0, 2, leaf_part, 0)
    pl.semaphore_wait(pltpu.get_barrier_semaphore(), jnp.where(x == z, 28, 42))

    for first, dst, send, recv in ((10, wy_v, wy_send, wy_recv), (8, wz_v, wz_send, wz_recv)):
        for d in (1, 3, 2):
            to = (z + d) % RING
            remote(weights.at[pl.ds(first, 2), RING * y + to], dst.at[z], send, recv, (y, x, to, core)).start()
        pltpu.make_async_copy(weights.at[pl.ds(first, 2), RING * y + z], dst.at[z], recv).start()
    lax.fori_loop(2, CHUNKS, leaf_part, 0)

    def forward_weights():
        pltpu.make_async_copy(wy_v, wy_v, wy_recv).wait()
        for d in (1, 3, 2):
            to = (x + d) % RING
            remote(wy_v.at[to], wx_v.at[x], wx_send, wx_recv, (y, to, z, core)).start()
        pltpu.make_async_copy(wy_v.at[x], wx_v.at[x], wx_recv).start()

    def mix_blocks(level, pairs):
        mixed = [
            mix(pair_weight(w_v[(level, *low)], w_v[(level, *high)]), c_v[low], c_v[high]) for low, high in pairs
        ]
        for (low, high), (first, second) in zip(pairs, mixed):
            c_v[low], c_v[high] = first, second

    for level in range(6):
        load_w(level).wait()
        spacing = 2**level

        def some(j, carry, level=level, spacing=spacing):
            pairs = []
            for u in range(BATCH):
                n = j * BATCH + u
                low = (n // spacing) * (2 * spacing) + n % spacing
                high = low + spacing
                pairs.append(((low // CHUNKS, low % CHUNKS), (high // CHUNKS, high % CHUNKS)))
            mix_blocks(level, pairs)
            return carry

        lax.fori_loop(0, GROUPS * CHUNKS // 2 // BATCH, some, 0)
    load_w(6).wait()
    load_w(7).wait()
    forward_weights()

    def send_core(k):
        return remote(c_v.at[:, k], sib_v.at[:, k], core_send.at[k], core_recv.at[k], (y, x, z, 1 - core))

    def level_6(k):
        mix_blocks(6, [((a, k), (a + GROUPS // 2, k)) for a in range(GROUPS // 2)])
        send_core(k).start()

    def level_7(k):
        send_core(k).wait_recv()

        mixed = [
            dot(w_v[7, a, k], jnp.concatenate([c_v[a, k], sib_v[a, k]], axis=0)).astype(BF16) for a in range(GROUPS)
        ]
        for a in range(GROUPS):
            e_v[a, k] = mixed[a]

    def send_z(k, half):
        part = pl.ds(half * HALF, HALF)
        there = pl.ds(pl.multiple_of(y * HALF, HALF), HALF)
        for d in (5, 7, 13, 15, 1, 3, 4, 12, 6, 9, 11, 14, 2, 8, 10):
            ty, tz = (y + d // RING) % RING, (z + d % RING) % RING
            remote(
                e_v.at[RING * ty + tz, k, :, part], z_v.at[k, half, z, :, there],
                z_send.at[k, half], z_recv.at[k, half], (ty, x, tz, core),
            ).start()
        mine = e_v.at[RING * y + z, k, :, part]
        pltpu.make_async_copy(mine, z_v.at[k, half, z, :, there], z_recv.at[k, half]).start()

    def two_levels(k, w, held):
        first = [pair_weight(w[b, 0, k], w[b + 1, 0, k]) for b in (0, 2)]
        second = [pair_weight(w[b, 1, k], w[b + 2, 1, k]) for b in (0, 1)]
        b0, b1 = mix(first[0], held[0], held[1])
        b2, b3 = mix(first[1], held[2], held[3])
        b0, b2 = mix(second[0], b0, b2)
        b1, b3 = mix(second[1], b1, b3)
        for b, value in enumerate((b0, b1, b2, b3)):
            held[b] = value

    def levels_z(k, half):
        held = z_v.at[k, half]
        pltpu.make_async_copy(held, held, z_recv.at[k, half]).wait()
        two_levels(k, wz_v, held)
        for d in (1, 3, 2):
            to = (x + d) % RING
            remote(held.at[to], x_v.at[k, half, x], x_send.at[k, half], x_recv.at[k, half], (y, to, z, core)).start()
        pltpu.make_async_copy(held.at[x], x_v.at[k, half, x], x_recv.at[k, half]).start()

    def levels_x(k, half):
        held = x_v.at[k, half]
        pltpu.make_async_copy(held, held, x_recv.at[k, half]).wait()
        two_levels(k, wx_v, held)

    def slowness(k):
        mine = RING * y + z
        rows = jnp.concatenate([x_v[k, half].reshape(RING * R2, RING * HALF) for half in range(2)], axis=1)
        for dy in (1, 3, 2, 0):
            part = (y + dy * turn) % RING
            total = dot(rows, table_v[:, pl.ds(pl.multiple_of(part * COLS, COLS), COLS)])
            s_v[k, :, part] = total.astype(BF16).reshape(RING, R2, COLS)
            for d in (1, 3, 2, 0):
                tx = (x + d * turn) % RING

                def send_back(tx=tx):
                    remote(s_v.at[k, tx, part], out.at[mine, k], back_send.at[k], back_recv.at[k], (part, tx, x, core)).start()

                if d == 0 and dy == 0:
                    pl.when(x != z)(send_back)

                    @pl.when(x == z)
                    def _():
                        pltpu.make_async_copy(s_v.at[k, x, part], out.at[mine, k], back_recv.at[k]).start()
                else:
                    send_back()

    def step(t, carry):
        now, before, last = t < CHUNKS, (t >= 2) & (t < CHUNKS + 2), t >= 3

        pl.when(now)(lambda: level_6(t))

        @pl.when((t >= 1) & (t < CHUNKS + 1))
        def _():
            level_7(t - 1)
            send_z(t - 1, 0)

        @pl.when(t == 2)
        def _():
            pltpu.make_async_copy(wz_v, wz_v, wz_recv).wait()

        pl.when(before)(lambda: levels_z(t - 2, 0))
        pl.when((t >= 1) & (t < CHUNKS + 1))(lambda: send_z(t - 1, 1))

        @pl.when(last)
        def _():
            levels_x(t - 3, 1)
            slowness(t - 3)

        pl.when(before)(lambda: levels_z(t - 2, 1))

        @pl.when(t == 2)
        def _():
            pltpu.make_async_copy(wx_v, wx_v, wx_recv).wait()
            pltpu.make_async_copy(table_v, table_v, table_sem).wait()

        pl.when(before)(lambda: levels_x(t - 2, 0))
        return carry

    lax.fori_loop(0, CHUNKS + 3, step, 0)

    def finish(k, carry):
        send_core(k).wait_send()
        for half in range(2):
            sent = e_v.at[pl.ds(0, 15), k, :, pl.ds(half * HALF, HALF)]
            pltpu.make_async_copy(sent, sent, z_send.at[k, half]).wait()
            sent = x_v.at[k, half, pl.ds(0, 3)]
            pltpu.make_async_copy(sent, sent, x_send.at[k, half]).wait()

        @pl.when(x != z)
        def _():
            pltpu.make_async_copy(s_v.at[k], s_v.at[k], back_send.at[k]).wait()

        @pl.when(x == z)
        def _():
            pltpu.make_async_copy(e_v.at[pl.ds(0, 15), k], e_v.at[pl.ds(0, 15), k], back_send.at[k]).wait()

        pltpu.make_async_copy(out.at[:, k], out.at[:, k], back_recv.at[k]).wait()
        return carry

    lax.fori_loop(0, CHUNKS, finish, 0)
    for held, sem in ((wy_v, wy_send), (wz_v, wz_send), (wx_v, wx_send)):
        pltpu.make_async_copy(held.at[pl.ds(0, 3)], held.at[pl.ds(0, 3)], sem).wait()


def model_kernel(basis, slow, out, basis_v, slow_v, out_v, basis_sem, slow_sem, out_sem):
    def piece(ref, p):
        return ref.at[pl.ds(p * PIECE, PIECE)]

    def load(p):
        return (
            pltpu.make_async_copy(piece(basis, p), piece(basis_v, p), basis_sem.at[p]),
            pltpu.make_async_copy(piece(slow, p), piece(slow_v, p), slow_sem.at[p]),
        )

    def store(p):
        return pltpu.make_async_copy(piece(out_v, p), piece(out, p), out_sem.at[p])

    pieces = basis.shape[0] // PIECE
    for p in range(pieces):
        for copy in load(p):
            copy.start()

    def some(p, carry):
        for copy in load(p):
            copy.wait()
        at = [p * PIECE + u for u in range(PIECE)]
        rows = [
            lax.dot_general(basis_v[n], slow_v[n], (((0,), (0,)), ((), ())), preferred_element_type=F32).astype(BF16)
            for n in at
        ]
        for u in range(PIECE):
            out_v[at[u]] = rows[u]
        store(p).start()
        return carry

    lax.fori_loop(0, pieces, some, 0)

    def finish(p, carry):
        store(p).wait()
        return carry

    lax.fori_loop(0, pieces, finish, 0)


def local(data, leaf_basis, level_weights, slowness_table, model_basis):
    any_space = pl.BlockSpec(memory_space=pl.ANY)
    levels = level_weights.shape[0]
    dma, vmem = pltpu.SemaphoreType.DMA, pltpu.VMEM
    slow = pl.pallas_call(
        main_kernel,
        out_shape=jax.ShapeDtypeStruct((GROUPS, CHUNKS, R2, COLS), BF16),
        in_specs=[any_space] * 4,
        out_specs=any_space,
        scratch_shapes=[
            vmem((GROUPS, CHUNKS, TB, COLS), BF16),
            vmem((GROUPS, CHUNKS, R2, TB), BF16),
            vmem((8, GROUPS, CHUNKS, R2, TB), BF16),
            vmem(slowness_table.shape, BF16),
            vmem((GROUPS, CHUNKS, R2, COLS), BF16),
            vmem((GROUPS, CHUNKS, R2, COLS), BF16),
            vmem((GROUPS, CHUNKS, R2, COLS), BF16),
            vmem((CHUNKS, 2, RING, R2, RING * HALF), BF16),
            vmem((CHUNKS, 2, RING, R2, RING * HALF), BF16),
            vmem((CHUNKS, RING, RING, R2, COLS), BF16),
            vmem((RING, 2, CHUNKS, R2, TB), BF16),
            vmem((RING, 2, CHUNKS, R2, TB), BF16),
            vmem((RING, 2, CHUNKS, R2, TB), BF16),
            dma((CHUNKS,)), dma((CHUNKS,)), dma((8,)), dma,
            dma, dma, dma, dma, dma, dma,
            dma((CHUNKS,)), dma((CHUNKS,)), dma((CHUNKS, 2)), dma((CHUNKS, 2)),
            dma((CHUNKS, 2)), dma((CHUNKS, 2)), dma((CHUNKS,)), dma((CHUNKS,)),
        ],
        compiler_params=pltpu.CompilerParams(collective_id=0, has_side_effects=True, vmem_limit_bytes=58 << 20),
    )(
        data.reshape(GROUPS, CHUNKS, TB, COLS),
        leaf_basis.reshape(GROUPS, CHUNKS, R2, TB),
        level_weights.reshape(levels, GROUPS, CHUNKS, R2, TB),
        slowness_table,
    )
    blocks = GROUPS * CHUNKS
    pieces = blocks // PIECE
    model = pl.pallas_call(
        model_kernel,
        out_shape=jax.ShapeDtypeStruct((blocks, TB, COLS), BF16),
        in_specs=[any_space] * 2,
        out_specs=any_space,
        scratch_shapes=[
            vmem((blocks, R2, TB), BF16), vmem((blocks, R2, COLS), BF16), vmem((blocks, TB, COLS), BF16),
            dma((pieces,)), dma((pieces,)), dma((pieces,)),
        ],
        compiler_params=pltpu.CompilerParams(vmem_limit_bytes=58 << 20),
    )(model_basis, slow.reshape(blocks, R2, COLS))
    return model.reshape(blocks * TB, COLS)


def solution(mesh):
    placed = (
        P("tm", "off"),
        P("tm", None, None),
        P(None, "tm", None, None),
        P(),
        P("tm", None, None),
    )
    return jax.shard_map(local, mesh=mesh, in_specs=placed, out_specs=P("tm", "off"), check_vma=False)
```
